768 devices in a mesh: grp: 12 (over z), rep: 64 (over y, x, core).
Axes of the slice: x: 4, y: 8, z: 12, core: 2. Of those that a mesh axis runs over, the one named last changes fastest.
Arguments:
- grid: bfloat16 [64, 12, 192, 512], P('rep', 'grp'), may hold values from -6 to 6
- cotangent: bfloat16 [64, 12, 192, 512], P('rep', 'grp'), may hold values from -6 to 6
- send_order: int32 [64, 12, 192], P('rep', 'grp'), may hold values from 0 to 191, each once within a row
- tile_nodes: int32 [64, 12, 24, 64], P('rep', 'grp'), may hold values from 0 to 191
- tile_edges: int32 [64, 12, 24, 64, 64], P('rep', 'grp'), may hold values 0 or 1
- tile_count: int32 [64, 12], P('rep', 'grp'), may hold values from 1 to 24, as said below
- w_first: bfloat16 [512, 512], replicated, may hold values from -0.25 to 0.25
- w_second: bfloat16 [512, 512], replicated, may hold values from -0.25 to 0.25
Outputs:
- grad_grid: bfloat16 [64, 12, 192, 512], P('rep', 'grp')
- grad_first: float32 [512, 512], replicated
- grad_second: float32 [512, 512], replicated
The draws below stay inside these ranges and needn't reach their ends.
Inputs may be any that keep to these rules, and one draw needn't show every extreme that they name: `tile_count`: every device uses at least one tile, and some device uses exactly 24.
All inputs are finite; a program needn't handle non-finite values. No bound on the sum of `tile_edges` on one device may be relied on, other than what follows from the above.
Results may differ from the reference program's by a relative error of at most 0.0055.
Values may be sent and summed in bfloat16 or wider, within the bound.
No kernel may reach another device: no remote copies, remote signals or barrier semaphores. Data moves between devices by JAX's collectives and lax.ppermute only.
A program may use at most 32 MiB of HBM per device.

```python
import jax
import jax.numpy as jnp
from jax import lax

D = 512
TILE = 64
NODE_DEV = 192
MAXB = 24
GROUPS = 64
PARTS_SIZE = 12


def draw_tile_count(key, part):
    key = jax.random.fold_in(key, 7)
    first, second = jax.random.split(key)
    counts = jax.random.randint(first, (GROUPS, PARTS_SIZE), 1, MAXB + 1)
    chosen = jax.random.randint(second, (), 0, GROUPS * PARTS_SIZE)
    places = jnp.arange(GROUPS * PARTS_SIZE).reshape(GROUPS, PARTS_SIZE)
    return jnp.where(places == chosen, MAXB, counts).astype(jnp.int32)


def touch_ends(drawn, rng, smallest, high):
    longest = drawn.shape.index(max(drawn.shape))
    spots = []
    for shift in (0, 1):
        where = [jax.random.randint(jax.random.fold_in(rng, axis), (), 0, length) for axis, length in enumerate(drawn.shape)]
        where[longest] = (where[longest] + shift) % drawn.shape[longest]
        spots.append(tuple(where))
    return drawn.at[spots[0]].set(smallest).at[spots[1]].set(high)


def block_scale(stream_key, extent, pieces, smallest, top_value):
    level = 1.0
    for position, parts in pieces:
        draws = jax.random.uniform(jax.random.fold_in(jax.random.fold_in(stream_key, 6), position), (parts,), jnp.float32, smallest / len(pieces), top_value / len(pieces))
        level = level * jnp.repeat(jnp.exp(draws), extent[position] // parts).reshape((-1,) + (1,) * (len(extent) - 1 - position))
    return level


def gaussian(own_key, extent, deviation, limit, shards=(), kind=jnp.bfloat16):
    result = deviation * jax.random.normal(own_key, extent, jnp.float32)
    if shards:
        result = result * block_scale(own_key, extent, shards, -0.22, 0.18)
    return jnp.clip(result, -limit, limit).astype(kind)


def setup_inputs(seed: int = 0) -> dict:
    streams_of = jax.random.split(jax.random.key(seed), 9)
    grid = gaussian(streams_of[0], (GROUPS, PARTS_SIZE, NODE_DEV, D), 1.0, 6.0, ((0, 64), (1, 12)))
    cotangent = gaussian(streams_of[1], (GROUPS, PARTS_SIZE, NODE_DEV, D), 1.0, 6.0, ((0, 64), (1, 12)))
    send_order = jax.vmap(lambda own: jax.random.permutation(own, NODE_DEV))(jax.random.split(streams_of[2], GROUPS * PARTS_SIZE)).reshape((GROUPS, PARTS_SIZE, NODE_DEV)).astype(jnp.int32)
    tile_nodes = touch_ends(jax.random.randint(streams_of[3], (GROUPS, PARTS_SIZE, MAXB, TILE), 0, NODE_DEV), jax.random.fold_in(streams_of[3], 1), 0, NODE_DEV - 1).astype(jnp.int32)
    tile_edges = touch_ends((jax.random.randint(streams_of[4], (GROUPS, PARTS_SIZE, MAXB, TILE, TILE), 0, 4) < 1).astype(jnp.int32), jax.random.fold_in(streams_of[4], 1), 0, 1)
    tile_count = draw_tile_count(jax.random.fold_in(streams_of[8], 71), 0)
    w_first = gaussian(streams_of[6], (D, D), D ** -0.5, 0.25)
    w_second = gaussian(streams_of[7], (D, D), D ** -0.5, 0.25)
    return dict(grid=grid, cotangent=cotangent, send_order=send_order, tile_nodes=tile_nodes, tile_edges=tile_edges, tile_count=tile_count, w_first=w_first, w_second=w_second)


def relayout(field):
    share = NODE_DEV // PARTS_SIZE
    blocks = field.reshape(GROUPS, PARTS_SIZE, PARTS_SIZE, share, D)
    return jnp.transpose(blocks, (0, 2, 1, 3, 4)).reshape(GROUPS, PARTS_SIZE, NODE_DEV, D)


def reference(grid, cotangent, send_order, tile_nodes, tile_edges, tile_count, w_first, w_second):
    hi = lax.Precision.HIGHEST
    sent = jnp.take_along_axis(grid, send_order[..., None].astype(jnp.int32), axis=2)
    part = relayout(sent)
    parts_flat = part.reshape(GROUPS * PARTS_SIZE, NODE_DEV, D)
    cot_flat = cotangent.reshape(GROUPS * PARTS_SIZE, NODE_DEV, D)
    nodes_flat = tile_nodes.reshape(GROUPS * PARTS_SIZE, MAXB, TILE)
    edges_flat = tile_edges.reshape(GROUPS * PARTS_SIZE, MAXB, TILE, TILE)
    count_flat = tile_count.reshape(GROUPS * PARTS_SIZE)

    def device(carry, item):
        rows, cots, nodes, edges, count = item

        def one_tile(b, inner):
            acc_first, acc_second, dpart = inner
            idx = lax.dynamic_index_in_dim(nodes, b, 0, keepdims=False).astype(jnp.int32)
            tile = lax.dynamic_index_in_dim(edges, b, 0, keepdims=False).astype(jnp.float32)
            hin = rows[idx]
            pre = jnp.dot(hin, w_first, preferred_element_type=jnp.float32)
            act = jax.nn.silu(pre).astype(jnp.bfloat16)
            agg = jnp.dot(tile, act.astype(jnp.float32), precision=hi).astype(jnp.bfloat16)
            dy = cots[idx]
            acc_second = acc_second + jnp.dot(agg.T, dy, preferred_element_type=jnp.float32)
            dagg = jnp.dot(dy, w_second.T, preferred_element_type=jnp.float32).astype(jnp.bfloat16)
            dact = jnp.dot(tile.T, dagg.astype(jnp.float32), precision=hi)
            sig = jax.nn.sigmoid(pre)
            dpre = (dact * sig * (1.0 + pre * (1.0 - sig))).astype(jnp.bfloat16)
            acc_first = acc_first + jnp.dot(hin.T, dpre, preferred_element_type=jnp.float32)
            dh = jnp.dot(dpre, w_first.T, preferred_element_type=jnp.float32)
            dpart = dpart.at[idx].add(dh)
            return acc_first, acc_second, dpart

        start = (carry[0], carry[1], jnp.zeros((NODE_DEV, D), jnp.float32))
        acc_first, acc_second, dpart = lax.fori_loop(jnp.int32(0), count.astype(jnp.int32), one_tile, start)
        return (acc_first, acc_second), dpart.astype(jnp.bfloat16)

    zero = jnp.zeros((D, D), jnp.float32)
    sums, dparts = lax.scan(device, (zero, zero), (parts_flat, cot_flat, nodes_flat, edges_flat, count_flat))
    back = relayout(dparts.reshape(GROUPS, PARTS_SIZE, NODE_DEV, D))
    order = send_order.astype(jnp.int32)
    g_idx = jnp.arange(GROUPS, dtype=jnp.int32)[:, None, None]
    p_idx = jnp.arange(PARTS_SIZE, dtype=jnp.int32)[None, :, None]
    grad_grid = jnp.zeros((GROUPS, PARTS_SIZE, NODE_DEV, D), jnp.bfloat16).at[g_idx, p_idx, order].set(back)
    factor = float(GROUPS * PARTS_SIZE * MAXB * TILE) ** -0.5
    return grad_grid, sums[0] * factor, sums[1] * factor
```

```python
import jax
import jax.numpy as jnp
from jax import lax
from jax.experimental import pallas as pl
from jax.experimental.pallas import tpu as pltpu
from jax.sharding import Mesh, PartitionSpec as P

BF = jnp.bfloat16
F32 = jnp.float32
NT = (((1,), (1,)), ((), ()))
TN = (((0,), (0,)), ((), ()))


def dot(a, b):
    return jnp.dot(a, b, preferred_element_type=F32)


def dot_nt(a, b):
    return lax.dot_general(a, b, NT, preferred_element_type=F32)


def dot_tn(a, b):
    return lax.dot_general(a, b, TN, preferred_element_type=F32)


def mark(hit):
    return jnp.where(hit, 1.0, 0.0).astype(BF)


def split(a):
    high = a.astype(BF)
    return high, (a - high.astype(F32)).astype(BF)


def send_kernel(order_ref, rows_ref, out_ref):
    n = rows_ref.shape[0]
    places = mark(lax.broadcasted_iota(jnp.int32, (n, n), 0) == order_ref[...])
    out_ref[...] = dot_tn(places, rows_ref[...]).astype(BF)


def local_kernel(count_ref, nodes_ref, edges_ref, cot_ref, w2_ref, high_ref, low_ref, t_ref):
    most, tile = nodes_ref.shape
    n = cot_ref.shape[0]
    count = count_ref[0, 0]
    ids = lax.broadcasted_iota(jnp.int32, (n, tile), 0)
    total = jnp.zeros((n, n), F32)
    for b in range(most):
        used = jnp.where(b < count, 1.0, 0.0)
        at = mark(ids == nodes_ref[b : b + 1, :])
        edges = (edges_ref[b].astype(F32) * used).astype(BF)
        total = total + dot_nt(dot(at, edges).astype(BF), at)
    high, low = split(total)
    high_ref[...] = high
    low_ref[...] = low
    dagg = dot_nt(cot_ref[...], w2_ref[...]).astype(BF)
    t_ref[...] = dot_tn(high, dagg) + dot_tn(low, dagg)


def node_kernel(factor, part_ref, w1_ref, cot_ref, high_ref, low_ref, t_ref, grads_ref, dpart_ref):
    d = w1_ref.shape[0]
    part = part_ref[...]
    pre = dot(part, w1_ref[...])
    sig = jax.nn.sigmoid(pre)
    act = (pre * sig).astype(BF)
    g = (t_ref[...] * sig * (1.0 + pre * (1.0 - sig))).astype(BF)
    dpart_ref[...] = dot_nt(g, w1_ref[...]).astype(BF)
    grads_ref[0:d, :] = (dot_tn(part, g) * factor).astype(BF)
    m = (dot(high_ref[...], act) + dot(low_ref[...], act)).astype(BF)
    grads_ref[d : 2 * d, :] = (dot_tn(m, cot_ref[...]) * factor).astype(BF)


def sum_kernel(pieces_ref, dpart_ref, both_ref):
    z, share, _ = dpart_ref.shape
    total = jnp.sum(pieces_ref[...].astype(F32), axis=0).astype(BF)
    for k in range(z):
        both_ref[k, 0:share, :] = dpart_ref[k]
        both_ref[k, share:, :] = total


def spread_kernel(both_ref, back_ref, whole_ref):
    z, share, _ = back_ref.shape
    back_ref[...] = both_ref[:, 0:share, :]
    total = jnp.sum(both_ref[:, share:, :].astype(F32), axis=0).astype(BF)
    for k in range(whole_ref.shape[0]):
        whole_ref[k] = total


def place_kernel(order_ref, back_ref, out_ref):
    n = back_ref.shape[0]
    places = mark(lax.broadcasted_iota(jnp.int32, (n, n), 0) == order_ref[...])
    out_ref[...] = dot(places, back_ref[...]).astype(BF)


def call(kernel, out_shape, flops, nbytes, *args, smem=0):
    specs = [pl.BlockSpec(memory_space=pltpu.SMEM)] * smem
    specs += [pl.BlockSpec(memory_space=pltpu.VMEM)] * (len(args) - smem)
    return pl.pallas_call(
        kernel,
        out_shape=out_shape,
        in_specs=specs,
        compiler_params=pltpu.CompilerParams(vmem_limit_bytes=32 * 1024 * 1024),
        cost_estimate=pl.CostEstimate(flops=flops, bytes_accessed=nbytes, transcendentals=0),
    )(*args)


def shards(grid, cotangent, send_order, tile_nodes, tile_edges, tile_count, w_first, w_second):
    rows, cot, order = grid[0, 0], cotangent[0, 0], send_order[0]
    nodes, edges = tile_nodes[0, 0], tile_edges[0, 0]
    z = lax.axis_size("grp")
    rep = lax.axis_size("rep")
    n, d = rows.shape
    most, tile = nodes.shape
    factor = float(z * rep * most * tile) ** -0.5
    sd = jax.ShapeDtypeStruct

    outgoing = call(send_kernel, sd((n, d), BF), 2 * n * n * d, 4 * n * d, order, rows)
    incoming = lax.all_to_all(outgoing.reshape(z, n // z, d), "grp", 0, 0, tiled=True)
    part = incoming.reshape(n, d)

    high, low, t = call(
        local_kernel,
        (sd((n, n), BF), sd((n, n), BF), sd((n, d), F32)),
        10**9, 6 * 10**6, tile_count, nodes, edges, cot, w_second, smem=1,
    )
    grads, dpart = call(
        lambda *refs: node_kernel(factor, *refs),
        (sd((2 * d, d), BF), sd((n, d), BF)),
        5 * 10**8, 3 * 10**6, part, w_first, cot, high, low, t,
    )

    share = 2 * d // rep
    pieces = lax.all_to_all(grads.reshape(rep, share, d), "rep", 0, 0, tiled=True)
    both = call(
        sum_kernel, sd((z, n // z + share, d), BF), 10**6, 2 * 10**6,
        pieces, dpart.reshape(z, n // z, d),
    )
    both = lax.all_to_all(both, "grp", 0, 0, tiled=True)
    back, whole = call(
        spread_kernel, (sd((z, n // z, d), BF), sd((rep, share, d), BF)), 10**6, 2 * 10**6, both
    )
    whole = lax.all_to_all(whole, "rep", 0, 0, tiled=True).reshape(2 * d, d)
    grad_rows = call(place_kernel, sd((n, d), BF), 2 * n * n * d, 4 * n * d, order, back.reshape(n, d))
    return (grad_rows[None, None], whole[:d].astype(F32), whole[d:].astype(F32))


def solution(mesh):
    in_specs = (
        P("rep", "grp", None, None),
        P("rep", "grp", None, None),
        P("rep", "grp", None),
        P("rep", "grp", None, None),
        P("rep", "grp", None, None, None),
        P("rep", "grp"),
        P(),
        P(),
    )
    out_specs = (P("rep", "grp", None, None), P(), P())
    return jax.shard_map(shards, mesh=mesh, in_specs=in_specs, out_specs=out_specs, check_vma=False)
```

```python
import jax
import jax.numpy as jnp
from jax import lax
from jax.experimental import pallas as pl
from jax.experimental.pallas import tpu as pltpu
from jax.sharding import Mesh, PartitionSpec as P

BF = jnp.bfloat16
F32 = jnp.float32
NT = (((1,), (1,)), ((), ()))
TN = (((0,), (0,)), ((), ()))


def dot(a, b):
    return jnp.dot(a, b, preferred_element_type=F32)


def dot_nt(a, b):
    return lax.dot_general(a, b, NT, preferred_element_type=F32)


def dot_tn(a, b):
    return lax.dot_general(a, b, TN, preferred_element_type=F32)


def mark(hit):
    return jnp.where(hit, 1.0, 0.0).astype(BF)


def split(a):
    high = a.astype(BF)
    return high, (a - high.astype(F32)).astype(BF)


def send_kernel(order_ref, rows_ref, out_ref):
    n = rows_ref.shape[0]
    places = mark(lax.broadcasted_iota(jnp.int32, (n, n), 0) == order_ref[...])
    out_ref[...] = dot_tn(places, rows_ref[...]).astype(BF)


def local_kernel(count_ref, nodes_ref, edges_ref, cot_ref, w2_ref, high_ref, low_ref, t_ref):
    most, tile = nodes_ref.shape
    n = cot_ref.shape[0]
    count = count_ref[0, 0]
    ids = lax.broadcasted_iota(jnp.int32, (n, tile), 0)
    total = jnp.zeros((n, n), F32)
    for b in range(most):
        used = jnp.where(b < count, 1.0, 0.0)
        at = mark(ids == nodes_ref[b : b + 1, :])
        edges = (edges_ref[b].astype(F32) * used).astype(BF)
        total = total + dot_nt(dot(at, edges).astype(BF), at)
    high, low = split(total)
    high_ref[...] = high
    low_ref[...] = low
    dagg = dot_nt(cot_ref[...], w2_ref[...]).astype(BF)
    t_ref[...] = dot_tn(high, dagg) + dot_tn(low, dagg)


def node_kernel(factor, core_ref, part_ref, w1_ref, cot_ref, high_ref, low_ref, t_ref, keep_ref, send_ref, dpart_ref):
    part = part_ref[...]
    pre = dot(part, w1_ref[...])
    sig = jax.nn.sigmoid(pre)
    act = (pre * sig).astype(BF)
    g = (t_ref[...] * sig * (1.0 + pre * (1.0 - sig))).astype(BF)
    m = (dot(high_ref[...], act) + dot(low_ref[...], act)).astype(BF)
    cot = cot_ref[...]
    zeroth = core_ref[0, 0] == 0

    @pl.when(zeroth)
    def _():
        send_ref[...] = (dot_tn(m, cot) * factor).astype(BF)
        keep_ref[...] = dot_tn(part, g) * factor

    @pl.when(jnp.logical_not(zeroth))
    def _():
        send_ref[...] = (dot_tn(part, g) * factor).astype(BF)
        keep_ref[...] = dot_tn(m, cot) * factor

    dpart_ref[...] = dot_nt(g, w1_ref[...]).astype(BF)


def add_kernel(keep_ref, got_ref, out_ref):
    out_ref[...] = (keep_ref[...] + got_ref[...].astype(F32)).astype(BF)


def sum_kernel(pieces_ref, dpart_ref, both_ref):
    z, share, _ = dpart_ref.shape
    total = jnp.sum(pieces_ref[...].astype(F32), axis=0).astype(BF)
    for k in range(z):
        both_ref[k, 0:share, :] = dpart_ref[k]
        both_ref[k, share:, :] = total


def spread_kernel(both_ref, back_ref, whole_ref):
    z, share, _ = back_ref.shape
    back_ref[...] = both_ref[:, 0:share, :]
    total = jnp.sum(both_ref[:, share:, :].astype(F32), axis=0).astype(BF)
    for k in range(whole_ref.shape[0]):
        whole_ref[k] = total


def place_kernel(order_ref, back_ref, out_ref):
    n = back_ref.shape[0]
    places = mark(lax.broadcasted_iota(jnp.int32, (n, n), 0) == order_ref[...])
    out_ref[...] = dot(places, back_ref[...]).astype(BF)


def final_kernel(core_ref, mine_ref, other_ref, first_ref, second_ref):
    zeroth = core_ref[0, 0] == 0
    mine, other = mine_ref[...].astype(F32), other_ref[...].astype(F32)
    first_ref[...] = jnp.where(zeroth, mine, other)
    second_ref[...] = jnp.where(zeroth, other, mine)


def call(kernel, out_shape, flops, nbytes, *args, smem=0):
    specs = [pl.BlockSpec(memory_space=pltpu.SMEM)] * smem
    specs += [pl.BlockSpec(memory_space=pltpu.VMEM)] * (len(args) - smem)
    return pl.pallas_call(
        kernel,
        out_shape=out_shape,
        in_specs=specs,
        compiler_params=pltpu.CompilerParams(vmem_limit_bytes=32 * 1024 * 1024),
        cost_estimate=pl.CostEstimate(flops=flops, bytes_accessed=nbytes, transcendentals=0),
    )(*args)


def shards(grid, cotangent, send_order, tile_nodes, tile_edges, tile_count, w_first, w_second):
    rows, cot, order = grid[0, 0], cotangent[0, 0], send_order[0]
    nodes, edges = tile_nodes[0, 0], tile_edges[0, 0]
    z = lax.axis_size("z")
    plane = lax.axis_size("y") * lax.axis_size("x")
    rep = plane * lax.axis_size("c")
    core = lax.axis_index("c").reshape(1, 1)
    swap = [(0, 1), (1, 0)]
    n, d = rows.shape
    most, tile = nodes.shape
    factor = float(z * rep * most * tile) ** -0.5
    sd = jax.ShapeDtypeStruct

    outgoing = call(send_kernel, sd((n, d), BF), 2 * n * n * d, 4 * n * d, order, rows)
    incoming = lax.all_to_all(outgoing.reshape(z, n // z, d), "z", 0, 0, tiled=True)
    part = incoming.reshape(n, d)

    high, low, t = call(
        local_kernel,
        (sd((n, n), BF), sd((n, n), BF), sd((n, d), F32)),
        10**9, 6 * 10**6, tile_count, nodes, edges, cot, w_second, smem=1,
    )
    keep, send, dpart = call(
        lambda *refs: node_kernel(factor, *refs),
        (sd((d, d), F32), sd((d, d), BF), sd((n, d), BF)),
        5 * 10**8, 3 * 10**6, core, part, w_first, cot, high, low, t, smem=1,
    )
    got = lax.ppermute(send, "c", swap)
    grad = call(add_kernel, sd((d, d), BF), 10**6, 2 * 10**6, keep, got)

    share = d // plane
    pieces = lax.all_to_all(grad.reshape(plane, share, d), ("y", "x"), 0, 0, tiled=True)
    both = call(
        sum_kernel, sd((z, n // z + share, d), BF), 10**6, 2 * 10**6,
        pieces, dpart.reshape(z, n // z, d),
    )
    both = lax.all_to_all(both, "z", 0, 0, tiled=True)
    back, whole = call(
        spread_kernel, (sd((z, n // z, d), BF), sd((plane, share, d), BF)), 10**6, 2 * 10**6, both
    )
    mine = lax.all_to_all(whole, ("y", "x"), 0, 0, tiled=True).reshape(d, d)
    grad_rows = call(
        place_kernel, sd((n, d), BF), 2 * n * n * d, 4 * n * d, order, back.reshape(n, d)
    )
    other = lax.ppermute(mine, "c", swap)
    first, second = call(
        final_kernel, (sd((d, d), F32), sd((d, d), F32)), 10**6, 3 * 10**6,
        core, mine, other, smem=1,
    )
    return (grad_rows[None, None], first, second)


def solution(mesh):
    z, rep = mesh.shape["grp"], mesh.shape["rep"]
    mesh = Mesh(mesh.devices.reshape(z, rep // 8, 4, 2), ("z", "y", "x", "c"))
    group = ("y", "x", "c")
    in_specs = (
        P(group, "z", None, None),
        P(group, "z", None, None),
        P(group, "z", None),
        P(group, "z", None, None),
        P(group, "z", None, None, None),
        P(group, "z"),
        P(),
        P(),
    )
    out_specs = (P(group, "z", None, None), P(), P())
    return jax.shard_map(shards, mesh=mesh, in_specs=in_specs, out_specs=out_specs, check_vma=False)
```

```python
import jax
import jax.numpy as jnp
from jax import lax
from jax.experimental import pallas as pl
from jax.experimental.pallas import tpu as pltpu
from jax.sharding import Mesh, PartitionSpec as P

BF = jnp.bfloat16
F32 = jnp.float32
NT = (((1,), (1,)), ((), ()))
TN = (((0,), (0,)), ((), ()))


def dot(a, b):
    return jnp.dot(a, b, preferred_element_type=F32)


def dot_nt(a, b):
    return lax.dot_general(a, b, NT, preferred_element_type=F32)


def dot_tn(a, b):
    return lax.dot_general(a, b, TN, preferred_element_type=F32)


def mark(hit):
    return jnp.where(hit, 1.0, 0.0).astype(BF)


def split(a):
    high = a.astype(BF)
    return high, (a - high.astype(F32)).astype(BF)


def send_kernel(order_hbm, rows_hbm, out_ref, order_ref, rows_ref, sems):
    order_copy = pltpu.make_async_copy(order_hbm, order_ref, sems.at[0])
    rows_copy = pltpu.make_async_copy(rows_hbm, rows_ref, sems.at[1])
    order_copy.start()
    rows_copy.start()
    order_copy.wait()
    n = rows_ref.shape[0]
    places = mark(lax.broadcasted_iota(jnp.int32, (n, n), 0) == order_ref[...])
    rows_copy.wait()
    out_ref[...] = dot_tn(places, rows_ref[...]).astype(BF)


def local_kernel(count_ref, nodes_ref, edges_ref, cot_ref, w2_ref, high_ref, low_ref, t_ref):
    most, tile = nodes_ref.shape
    n = cot_ref.shape[0]
    count = count_ref[0, 0]
    ids = lax.broadcasted_iota(jnp.int32, (n, tile), 0)
    total = jnp.zeros((n, n), F32)
    for b in range(most):
        used = jnp.where(b < count, 1.0, 0.0)
        at = mark(ids == nodes_ref[b : b + 1, :])
        edges = (edges_ref[b].astype(F32) * used).astype(BF)
        total = total + dot_nt(dot(at, edges).astype(BF), at)
    high, low = split(total)
    high_ref[...] = high
    low_ref[...] = low
    dagg = dot_nt(cot_ref[...], w2_ref[...]).astype(BF)
    t_ref[...] = dot_tn(high, dagg) + dot_tn(low, dagg)


def node_kernel(factor, core_ref, part_ref, w1_ref, cot_ref, high_ref, low_ref, t_ref, keep_ref, send_ref, dpart_ref):
    part = part_ref[...]
    pre = dot(part, w1_ref[...])
    sig = jax.nn.sigmoid(pre)
    act = (pre * sig).astype(BF)
    g = (t_ref[...] * sig * (1.0 + pre * (1.0 - sig))).astype(BF)
    m = (dot(high_ref[...], act) + dot(low_ref[...], act)).astype(BF)
    cot = cot_ref[...]
    zeroth = core_ref[0, 0] == 0

    @pl.when(zeroth)
    def _():
        send_ref[...] = (dot_tn(m, cot) * factor).astype(BF)
        keep_ref[...] = dot_tn(part, g) * factor

    @pl.when(jnp.logical_not(zeroth))
    def _():
        send_ref[...] = (dot_tn(part, g) * factor).astype(BF)
        keep_ref[...] = dot_tn(m, cot) * factor

    dpart_ref[...] = dot_nt(g, w1_ref[...]).astype(BF)


def add_kernel(keep_ref, got_ref, out_ref):
    nx, ny, share, _ = out_ref.shape
    for y in range(ny):
        for x in range(nx):
            at = pl.ds((y * nx + x) * share, share)
            out_ref[x, y] = (keep_ref[at, :] + got_ref[at, :].astype(F32)).astype(BF)


def sum_x_kernel(pieces_ref, out_ref):
    out_ref[...] = jnp.sum(pieces_ref[...].astype(F32), axis=0).astype(BF)


def sum_kernel(pieces_ref, dpart_ref, both_ref):
    z, share, _ = dpart_ref.shape
    total = jnp.sum(pieces_ref[...].astype(F32), axis=0).astype(BF)
    for k in range(z):
        both_ref[k, 0:share, :] = dpart_ref[k]
        both_ref[k, share:, :] = total


def spread_kernel(both_ref, back_ref, whole_ref):
    z, share, _ = back_ref.shape
    back_ref[...] = both_ref[:, 0:share, :]
    total = jnp.sum(both_ref[:, share:, :].astype(F32), axis=0).astype(BF)
    for k in range(whole_ref.shape[0]):
        whole_ref[k] = total


def place_kernel(order_ref, back_ref, out_ref):
    n = back_ref.shape[0]
    places = mark(lax.broadcasted_iota(jnp.int32, (n, n), 0) == order_ref[...])
    out_ref[...] = dot(places, back_ref[...]).astype(BF)


def final_kernel(core_ref, mine_ref, other_ref, first_ref, second_ref):
    zeroth = core_ref[0, 0] == 0
    mine, other = mine_ref[...].astype(F32), other_ref[...].astype(F32)
    first_ref[...] = jnp.where(zeroth, mine, other)
    second_ref[...] = jnp.where(zeroth, other, mine)


def call(kernel, out_shape, flops, nbytes, *args, smem=0):
    specs = [pl.BlockSpec(memory_space=pltpu.SMEM)] * smem
    specs += [pl.BlockSpec(memory_space=pltpu.VMEM)] * (len(args) - smem)
    return pl.pallas_call(
        kernel,
        out_shape=out_shape,
        in_specs=specs,
        compiler_params=pltpu.CompilerParams(vmem_limit_bytes=32 * 1024 * 1024),
        cost_estimate=pl.CostEstimate(flops=flops, bytes_accessed=nbytes, transcendentals=0),
    )(*args)


def shards(grid, cotangent, send_order, tile_nodes, tile_edges, tile_count, w_first, w_second):
    rows, cot, order = grid[0, 0], cotangent[0, 0], send_order[0]
    nodes, edges = tile_nodes[0, 0], tile_edges[0, 0]
    z = lax.axis_size("z")
    plane = lax.axis_size("y") * lax.axis_size("x")
    rep = plane * lax.axis_size("c")
    core = lax.axis_index("c").reshape(1, 1)
    swap = [(0, 1), (1, 0)]
    n, d = rows.shape
    most, tile = nodes.shape
    factor = float(z * rep * most * tile) ** -0.5
    sd = jax.ShapeDtypeStruct

    outgoing = pl.pallas_call(
        send_kernel,
        out_shape=sd((n, d), BF),
        in_specs=[pl.BlockSpec(memory_space=pl.ANY)] * 2,
        out_specs=pl.BlockSpec(memory_space=pltpu.VMEM),
        scratch_shapes=[
            pltpu.VMEM((1, n), jnp.int32),
            pltpu.VMEM((n, d), BF),
            pltpu.SemaphoreType.DMA((2,)),
        ],
    )(order, rows)
    incoming = lax.all_to_all(outgoing.reshape(z, n // z, d), "z", 0, 0, tiled=True)
    part = incoming.reshape(n, d)

    high, low, t = call(
        local_kernel,
        (sd((n, n), BF), sd((n, n), BF), sd((n, d), F32)),
        10**9, 6 * 10**6, tile_count, nodes, edges, cot, w_second, smem=1,
    )
    keep, send, dpart = call(
        lambda *refs: node_kernel(factor, *refs),
        (sd((d, d), F32), sd((d, d), BF), sd((n, d), BF)),
        5 * 10**8, 3 * 10**6, core, part, w_first, cot, high, low, t, smem=1,
    )
    got = lax.ppermute(send, "c", swap)
    nx = lax.axis_size("x")
    share = d // plane
    grad = call(
        add_kernel, sd((nx, plane // nx, share, d), BF), 10**6, 2 * 10**6, keep, got
    )
    grad = lax.all_to_all(grad.reshape(nx, d // nx, d), "x", 0, 0, tiled=True)
    grad = call(sum_x_kernel, sd((d // nx, d), BF), 10**6, 10**6, grad)
    pieces = lax.all_to_all(grad.reshape(plane // nx, share, d), "y", 0, 0, tiled=True)
    both = call(
        sum_kernel, sd((z, n // z + share, d), BF), 10**6, 2 * 10**6,
        pieces, dpart.reshape(z, n // z, d),
    )
    both = lax.all_to_all(both, "z", 0, 0, tiled=True)
    back, whole = call(
        spread_kernel, (sd((z, n // z, d), BF), sd((plane, share, d), BF)), 10**6, 2 * 10**6, both
    )
    mine = lax.all_to_all(whole, ("y", "x"), 0, 0, tiled=True).reshape(d, d)
    grad_rows = call(
        place_kernel, sd((n, d), BF), 2 * n * n * d, 4 * n * d, order, back.reshape(n, d)
    )
    other = lax.ppermute(mine, "c", swap)
    first, second = call(
        final_kernel, (sd((d, d), F32), sd((d, d), F32)), 10**6, 3 * 10**6,
        core, mine, other, smem=1,
    )
    return (grad_rows[None, None], first, second)


def solution(mesh):
    z, rep = mesh.shape["grp"], mesh.shape["rep"]
    mesh = Mesh(mesh.devices.reshape(z, rep // 8, 4, 2), ("z", "y", "x", "c"))
    group = ("y", "x", "c")
    in_specs = (
        P(group, "z", None, None),
        P(group, "z", None, None),
        P(group, "z", None),
        P(group, "z", None, None),
        P(group, "z", None, None, None),
        P(group, "z"),
        P(),
        P(),
    )
    out_specs = (P(group, "z", None, None), P(), P())
    return jax.shard_map(shards, mesh=mesh, in_specs=in_specs, out_specs=out_specs, check_vma=False)
```

```python
import jax
import jax.numpy as jnp
from jax import lax
from jax.experimental import pallas as pl
from jax.experimental.pallas import tpu as pltpu
from jax.sharding import Mesh, PartitionSpec as P

BF = jnp.bfloat16
F32 = jnp.float32
STRIDE = 7
NT = (((1,), (1,)), ((), ()))
TN = (((0,), (0,)), ((), ()))


def dot(a, b):
    return jnp.dot(a, b, preferred_element_type=F32)


def dot_nt(a, b):
    return lax.dot_general(a, b, NT, preferred_element_type=F32)


def dot_tn(a, b):
    return lax.dot_general(a, b, TN, preferred_element_type=F32)


def mark(hit):
    return jnp.where(hit, 1.0, 0.0).astype(BF)


def split(a):
    high = a.astype(BF)
    return high, (a - high.astype(F32)).astype(BF)


def along_z(z):
    return [STRIDE * k % z for k in range(z)]


def in_order(blocks_ref):
    z = blocks_ref.shape[0]
    places = along_z(z)
    return jnp.concatenate([blocks_ref[places.index(k)] for k in range(z)], axis=0)


def exchange_z(blocks):
    return lax.all_to_all(
        blocks, "z", 0, 0, tiled=True, axis_index_groups=[along_z(blocks.shape[0])]
    )


def send_kernel(order_hbm, rows_hbm, out_ref, order_ref, rows_ref, sems):
    order_copy = pltpu.make_async_copy(order_hbm, order_ref, sems.at[0])
    rows_copy = pltpu.make_async_copy(rows_hbm, rows_ref, sems.at[1])
    order_copy.start()
    rows_copy.start()
    order_copy.wait()
    n = rows_ref.shape[0]
    places = mark(lax.broadcasted_iota(jnp.int32, (n, n), 0) == order_ref[...])
    rows_copy.wait()
    sent = dot_tn(places, rows_ref[...]).astype(BF)
    z, share, _ = out_ref.shape
    for k, device in enumerate(along_z(z)):
        out_ref[k] = sent[device * share : (device + 1) * share]


def local_kernel(count_ref, nodes_ref, edges_ref, cot_ref, w2_ref, high_ref, low_ref, t_ref):
    most, tile = nodes_ref.shape
    n = cot_ref.shape[0]
    count = count_ref[0, 0]
    ids = lax.broadcasted_iota(jnp.int32, (n, tile), 0)
    total = jnp.zeros((n, n), F32)
    for b in range(most):
        used = jnp.where(b < count, 1.0, 0.0)
        at = mark(ids == nodes_ref[b : b + 1, :])
        edges = (edges_ref[b].astype(F32) * used).astype(BF)
        total = total + dot_nt(dot(at, edges).astype(BF), at)
    high, low = split(total)
    high_ref[...] = high
    low_ref[...] = low
    dagg = dot_nt(cot_ref[...], w2_ref[...]).astype(BF)
    t_ref[...] = dot_tn(high, dagg) + dot_tn(low, dagg)


def node_kernel(factor, core_ref, part_ref, w1_ref, cot_ref, high_ref, low_ref, t_ref, send_ref, g_ref, m_ref):
    part = in_order(part_ref)
    pre = dot(part, w1_ref[...])
    sig = jax.nn.sigmoid(pre)
    act = (pre * sig).astype(BF)
    g = (t_ref[...] * sig * (1.0 + pre * (1.0 - sig))).astype(BF)
    m = (dot(high_ref[...], act) + dot(low_ref[...], act)).astype(BF)
    g_ref[...] = g
    m_ref[...] = m
    zeroth = core_ref[0, 0] == 0

    @pl.when(zeroth)
    def _():
        send_ref[...] = (dot_tn(m, cot_ref[...]) * factor).astype(BF)

    @pl.when(jnp.logical_not(zeroth))
    def _():
        send_ref[...] = (dot_tn(part, g) * factor).astype(BF)


def keep_kernel(factor, core_ref, part_ref, w1_ref, cot_ref, g_ref, m_ref, keep_ref, dpart_ref):
    zeroth = core_ref[0, 0] == 0
    g = g_ref[...]

    @pl.when(zeroth)
    def _():
        keep_ref[...] = dot_tn(in_order(part_ref), g) * factor

    @pl.when(jnp.logical_not(zeroth))
    def _():
        keep_ref[...] = dot_tn(m_ref[...], cot_ref[...]) * factor

    dpart_ref[...] = dot_nt(g, w1_ref[...]).astype(BF)


def add_kernel(keep_ref, got_ref, out_ref):
    nx, ny, share, _ = out_ref.shape
    for y in range(ny):
        for x in range(nx):
            at = pl.ds((y * nx + x) * share, share)
            out_ref[x, y] = (keep_ref[at, :] + got_ref[at, :].astype(F32)).astype(BF)


def sum_x_kernel(pieces_ref, out_ref):
    out_ref[...] = jnp.sum(pieces_ref[...].astype(F32), axis=0).astype(BF)


def sum_kernel(pieces_ref, dpart_ref, both_ref):
    z, share, _ = dpart_ref.shape
    total = jnp.sum(pieces_ref[...].astype(F32), axis=0).astype(BF)
    for k, device in enumerate(along_z(z)):
        both_ref[k, 0:share, :] = dpart_ref[device]
        both_ref[k, share:, :] = total


def spread_kernel(both_ref, back_ref, whole_ref):
    z, share, _ = back_ref.shape
    for k, device in enumerate(along_z(z)):
        back_ref[device] = both_ref[k, 0:share, :]
    total = jnp.sum(both_ref[:, share:, :].astype(F32), axis=0).astype(BF)
    for k in range(whole_ref.shape[0]):
        whole_ref[k] = total


def place_kernel(order_ref, back_ref, out_ref):
    n = back_ref.shape[0]
    places = mark(lax.broadcasted_iota(jnp.int32, (n, n), 0) == order_ref[...])
    out_ref[...] = dot(places, back_ref[...]).astype(BF)


def final_kernel(core_ref, mine_ref, other_ref, first_ref, second_ref):
    zeroth = core_ref[0, 0] == 0
    mine, other = mine_ref[...].astype(F32), other_ref[...].astype(F32)
    first_ref[...] = jnp.where(zeroth, mine, other)
    second_ref[...] = jnp.where(zeroth, other, mine)


def call(kernel, out_shape, flops, nbytes, *args, smem=0):
    specs = [pl.BlockSpec(memory_space=pltpu.SMEM)] * smem
    specs += [pl.BlockSpec(memory_space=pltpu.VMEM)] * (len(args) - smem)
    return pl.pallas_call(
        kernel,
        out_shape=out_shape,
        in_specs=specs,
        compiler_params=pltpu.CompilerParams(vmem_limit_bytes=32 * 1024 * 1024),
        cost_estimate=pl.CostEstimate(flops=flops, bytes_accessed=nbytes, transcendentals=0),
    )(*args)


def shards(grid, cotangent, send_order, tile_nodes, tile_edges, tile_count, w_first, w_second):
    rows, cot, order = grid[0, 0], cotangent[0, 0], send_order[0]
    nodes, edges = tile_nodes[0, 0], tile_edges[0, 0]
    z = lax.axis_size("z")
    plane = lax.axis_size("y") * lax.axis_size("x")
    rep = plane * lax.axis_size("c")
    core = lax.axis_index("c").reshape(1, 1)
    swap = [(0, 1), (1, 0)]
    n, d = rows.shape
    most, tile = nodes.shape
    factor = float(z * rep * most * tile) ** -0.5
    sd = jax.ShapeDtypeStruct

    outgoing = pl.pallas_call(
        send_kernel,
        out_shape=sd((z, n // z, d), BF),
        in_specs=[pl.BlockSpec(memory_space=pl.ANY)] * 2,
        out_specs=pl.BlockSpec(memory_space=pltpu.VMEM),
        scratch_shapes=[
            pltpu.VMEM((1, n), jnp.int32),
            pltpu.VMEM((n, d), BF),
            pltpu.SemaphoreType.DMA((2,)),
        ],
    )(order, rows)
    part = exchange_z(outgoing)

    high, low, t = call(
        local_kernel,
        (sd((n, n), BF), sd((n, n), BF), sd((n, d), F32)),
        10**9, 6 * 10**6, tile_count, nodes, edges, cot, w_second, smem=1,
    )
    send, g, m = call(
        lambda *refs: node_kernel(factor, *refs),
        (sd((d, d), BF), sd((n, d), BF), sd((n, d), BF)),
        4 * 10**8, 3 * 10**6, core, part, w_first, cot, high, low, t, smem=1,
    )
    got = lax.ppermute(send, "c", swap)
    keep, dpart = call(
        lambda *refs: keep_kernel(factor, *refs),
        (sd((d, d), F32), sd((n, d), BF)),
        2 * 10**8, 3 * 10**6, core, part, w_first, cot, g, m, smem=1,
    )
    nx = lax.axis_size("x")
    share = d // plane
    grad = call(
        add_kernel, sd((nx, plane // nx, share, d), BF), 10**6, 2 * 10**6, keep, got
    )
    grad = lax.all_to_all(grad.reshape(nx, d // nx, d), "x", 0, 0, tiled=True)
    grad = call(sum_x_kernel, sd((d // nx, d), BF), 10**6, 10**6, grad)
    pieces = lax.all_to_all(grad.reshape(plane // nx, share, d), "y", 0, 0, tiled=True)
    both = call(
        sum_kernel, sd((z, n // z + share, d), BF), 10**6, 2 * 10**6,
        pieces, dpart.reshape(z, n // z, d),
    )
    both = exchange_z(both)
    back, whole = call(
        spread_kernel, (sd((z, n // z, d), BF), sd((plane, share, d), BF)), 10**6, 2 * 10**6, both
    )
    mine = lax.all_to_all(whole, ("y", "x"), 0, 0, tiled=True).reshape(d, d)
    grad_rows = call(
        place_kernel, sd((n, d), BF), 2 * n * n * d, 4 * n * d, order, back.reshape(n, d)
    )
    other = lax.ppermute(mine, "c", swap)
    first, second = call(
        final_kernel, (sd((d, d), F32), sd((d, d), F32)), 10**6, 3 * 10**6,
        core, mine, other, smem=1,
    )
    return (grad_rows[None, None], first, second)


def solution(mesh):
    z, rep = mesh.shape["grp"], mesh.shape["rep"]
    mesh = Mesh(mesh.devices.reshape(z, rep // 8, 4, 2), ("z", "y", "x", "c"))
    group = ("y", "x", "c")
    in_specs = (
        P(group, "z", None, None),
        P(group, "z", None, None),
        P(group, "z", None),
        P(group, "z", None, None),
        P(group, "z", None, None, None),
        P(group, "z"),
        P(),
        P(),
    )
    out_specs = (P(group, "z", None, None), P(), P())
    return jax.shard_map(shards, mesh=mesh, in_specs=in_specs, out_specs=out_specs, check_vma=False)
```

```python
import jax
import jax.numpy as jnp
from jax import lax
from jax.experimental import pallas as pl
from jax.experimental.pallas import tpu as pltpu
from jax.sharding import Mesh, PartitionSpec as P

BF = jnp.bfloat16
F32 = jnp.float32
NT = (((1,), (1,)), ((), ()))
TN = (((0,), (0,)), ((), ()))


def dot(a, b):
    return jnp.dot(a, b, preferred_element_type=F32)


def dot_nt(a, b):
    return lax.dot_general(a, b, NT, preferred_element_type=F32)


def dot_tn(a, b):
    return lax.dot_general(a, b, TN, preferred_element_type=F32)


def mark(hit):
    return jnp.where(hit, 1.0, 0.0).astype(BF)


def split(a):
    high = a.astype(BF)
    return high, (a - high.astype(F32)).astype(BF)


def along_z(z):
    half = (z + 1) // 2
    return [k % 2 * half + k // 2 for k in range(z)]


def in_order(blocks_ref):
    z = blocks_ref.shape[0]
    places = along_z(z)
    return jnp.concatenate([blocks_ref[places.index(k)] for k in range(z)], axis=0)


def exchange_z(blocks):
    return lax.all_to_all(
        blocks, "z", 0, 0, tiled=True, axis_index_groups=[along_z(blocks.shape[0])]
    )


def send_kernel(order_hbm, rows_hbm, out_ref, order_ref, rows_ref, sems):
    order_copy = pltpu.make_async_copy(order_hbm, order_ref, sems.at[0])
    rows_copy = pltpu.make_async_copy(rows_hbm, rows_ref, sems.at[1])
    order_copy.start()
    rows_copy.start()
    order_copy.wait()
    n = rows_ref.shape[0]
    places = mark(lax.broadcasted_iota(jnp.int32, (n, n), 0) == order_ref[...])
    rows_copy.wait()
    sent = dot_tn(places, rows_ref[...]).astype(BF)
    z, share, _ = out_ref.shape
    for k, device in enumerate(along_z(z)):
        out_ref[k] = sent[device * share : (device + 1) * share]


def local_kernel(count_ref, nodes_ref, edges_ref, cot_ref, w2_ref, high_ref, low_ref, t_ref):
    most, tile = nodes_ref.shape
    n = cot_ref.shape[0]
    count = count_ref[0, 0]
    ids = lax.broadcasted_iota(jnp.int32, (n, tile), 0)
    total = jnp.zeros((n, n), F32)
    for b in range(most):
        used = jnp.where(b < count, 1.0, 0.0)
        at = mark(ids == nodes_ref[b : b + 1, :])
        edges = (edges_ref[b].astype(F32) * used).astype(BF)
        total = total + dot_nt(dot(at, edges).astype(BF), at)
    high, low = split(total)
    high_ref[...] = high
    low_ref[...] = low
    dagg = dot_nt(cot_ref[...], w2_ref[...]).astype(BF)
    t_ref[...] = dot_tn(high, dagg) + dot_tn(low, dagg)


def node_kernel(factor, core_ref, part_ref, w1_ref, cot_ref, high_ref, low_ref, t_ref, send_ref, g_ref, m_ref):
    part = in_order(part_ref)
    pre = dot(part, w1_ref[...])
    sig = jax.nn.sigmoid(pre)
    act = (pre * sig).astype(BF)
    g = (t_ref[...] * sig * (1.0 + pre * (1.0 - sig))).astype(BF)
    m = (dot(high_ref[...], act) + dot(low_ref[...], act)).astype(BF)
    g_ref[...] = g
    m_ref[...] = m
    zeroth = core_ref[0, 0] == 0

    @pl.when(zeroth)
    def _():
        send_ref[...] = (dot_tn(m, cot_ref[...]) * factor).astype(BF)

    @pl.when(jnp.logical_not(zeroth))
    def _():
        send_ref[...] = (dot_tn(part, g) * factor).astype(BF)


def keep_kernel(factor, core_ref, part_ref, w1_ref, cot_ref, g_ref, m_ref, keep_ref, dpart_ref):
    zeroth = core_ref[0, 0] == 0
    g = g_ref[...]

    @pl.when(zeroth)
    def _():
        keep_ref[...] = dot_tn(in_order(part_ref), g) * factor

    @pl.when(jnp.logical_not(zeroth))
    def _():
        keep_ref[...] = dot_tn(m_ref[...], cot_ref[...]) * factor

    dpart_ref[...] = dot_nt(g, w1_ref[...]).astype(BF)


def add_kernel(keep_ref, got_ref, out_ref):
    nx, ny, share, _ = out_ref.shape
    for y in range(ny):
        for x in range(nx):
            at = pl.ds((y * nx + x) * share, share)
            out_ref[x, y] = (keep_ref[at, :] + got_ref[at, :].astype(F32)).astype(BF)


def sum_x_kernel(pieces_ref, out_ref):
    out_ref[...] = jnp.sum(pieces_ref[...].astype(F32), axis=0).astype(BF)


def sum_kernel(pieces_ref, dpart_ref, both_ref):
    z, share, _ = dpart_ref.shape
    total = jnp.sum(pieces_ref[...].astype(F32), axis=0).astype(BF)
    for k, device in enumerate(along_z(z)):
        both_ref[k, 0:share, :] = dpart_ref[device]
        both_ref[k, share:, :] = total


def spread_kernel(both_ref, back_ref, whole_ref):
    z, share, _ = back_ref.shape
    for k, device in enumerate(along_z(z)):
        back_ref[device] = both_ref[k, 0:share, :]
    total = jnp.sum(both_ref[:, share:, :].astype(F32), axis=0).astype(BF)
    for k in range(whole_ref.shape[0]):
        whole_ref[k] = total


def place_kernel(order_ref, back_ref, out_ref):
    n = back_ref.shape[0]
    places = mark(lax.broadcasted_iota(jnp.int32, (n, n), 0) == order_ref[...])
    out_ref[...] = dot(places, back_ref[...]).astype(BF)


def final_kernel(core_ref, mine_ref, other_ref, first_ref, second_ref):
    zeroth = core_ref[0, 0] == 0
    mine, other = mine_ref[...].astype(F32), other_ref[...].astype(F32)
    first_ref[...] = jnp.where(zeroth, mine, other)
    second_ref[...] = jnp.where(zeroth, other, mine)


def call(kernel, out_shape, flops, nbytes, *args, smem=0):
    specs = [pl.BlockSpec(memory_space=pltpu.SMEM)] * smem
    specs += [pl.BlockSpec(memory_space=pltpu.VMEM)] * (len(args) - smem)
    return pl.pallas_call(
        kernel,
        out_shape=out_shape,
        in_specs=specs,
        compiler_params=pltpu.CompilerParams(vmem_limit_bytes=32 * 1024 * 1024),
        cost_estimate=pl.CostEstimate(flops=flops, bytes_accessed=nbytes, transcendentals=0),
    )(*args)


def shards(grid, cotangent, send_order, tile_nodes, tile_edges, tile_count, w_first, w_second):
    rows, cot, order = grid[0, 0], cotangent[0, 0], send_order[0]
    nodes, edges = tile_nodes[0, 0], tile_edges[0, 0]
    z = lax.axis_size("z")
    plane = lax.axis_size("y") * lax.axis_size("x")
    rep = plane * lax.axis_size("c")
    core = lax.axis_index("c").reshape(1, 1)
    swap = [(0, 1), (1, 0)]
    n, d = rows.shape
    most, tile = nodes.shape
    factor = float(z * rep * most * tile) ** -0.5
    sd = jax.ShapeDtypeStruct

    outgoing = pl.pallas_call(
        send_kernel,
        out_shape=sd((z, n // z, d), BF),
        in_specs=[pl.BlockSpec(memory_space=pl.ANY)] * 2,
        out_specs=pl.BlockSpec(memory_space=pltpu.VMEM),
        scratch_shapes=[
            pltpu.VMEM((1, n), jnp.int32),
            pltpu.VMEM((n, d), BF),
            pltpu.SemaphoreType.DMA((2,)),
        ],
    )(order, rows)
    part = exchange_z(outgoing)

    high, low, t = call(
        local_kernel,
        (sd((n, n), BF), sd((n, n), BF), sd((n, d), F32)),
        10**9, 6 * 10**6, tile_count, nodes, edges, cot, w_second, smem=1,
    )
    send, g, m = call(
        lambda *refs: node_kernel(factor, *refs),
        (sd((d, d), BF), sd((n, d), BF), sd((n, d), BF)),
        4 * 10**8, 3 * 10**6, core, part, w_first, cot, high, low, t, smem=1,
    )
    got = lax.ppermute(send, "c", swap)
    keep, dpart = call(
        lambda *refs: keep_kernel(factor, *refs),
        (sd((d, d), F32), sd((n, d), BF)),
        2 * 10**8, 3 * 10**6, core, part, w_first, cot, g, m, smem=1,
    )
    nx = lax.axis_size("x")
    share = d // plane
    grad = call(
        add_kernel, sd((nx, plane // nx, share, d), BF), 10**6, 2 * 10**6, keep, got
    )
    grad = lax.all_to_all(grad.reshape(nx, d // nx, d), "x", 0, 0, tiled=True)
    grad = call(sum_x_kernel, sd((d // nx, d), BF), 10**6, 10**6, grad)
    pieces = lax.all_to_all(grad.reshape(plane // nx, share, d), "y", 0, 0, tiled=True)
    both = call(
        sum_kernel, sd((z, n // z + share, d), BF), 10**6, 2 * 10**6,
        pieces, dpart.reshape(z, n // z, d),
    )
    both = exchange_z(both)
    back, whole = call(
        spread_kernel, (sd((z, n // z, d), BF), sd((plane, share, d), BF)), 10**6, 2 * 10**6, both
    )
    mine = lax.all_to_all(whole, ("y", "x"), 0, 0, tiled=True).reshape(d, d)
    grad_rows = call(
        place_kernel, sd((n, d), BF), 2 * n * n * d, 4 * n * d, order, back.reshape(n, d)
    )
    other = lax.ppermute(mine, "c", swap)
    first, second = call(
        final_kernel, (sd((d, d), F32), sd((d, d), F32)), 10**6, 3 * 10**6,
        core, mine, other, smem=1,
    )
    return (grad_rows[None, None], first, second)


def solution(mesh):
    z, rep = mesh.shape["grp"], mesh.shape["rep"]
    mesh = Mesh(mesh.devices.reshape(z, rep // 8, 4, 2), ("z", "y", "x", "c"))
    group = ("y", "x", "c")
    in_specs = (
        P(group, "z", None, None),
        P(group, "z", None, None),
        P(group, "z", None),
        P(group, "z", None, None),
        P(group, "z", None, None, None),
        P(group, "z"),
        P(),
        P(),
    )
    out_specs = (P(group, "z", None, None), P(), P())
    return jax.shard_map(shards, mesh=mesh, in_specs=in_specs, out_specs=out_specs, check_vma=False)
```

```python
import jax
import jax.numpy as jnp
from jax import lax
from jax.experimental import pallas as pl
from jax.experimental.pallas import tpu as pltpu
from jax.sharding import Mesh, PartitionSpec as P

BF = jnp.bfloat16
F32 = jnp.float32
NT = (((1,), (1,)), ((), ()))
TN = (((0,), (0,)), ((), ()))


def dot(a, b):
    return jnp.dot(a, b, preferred_element_type=F32)


def dot_nt(a, b):
    return lax.dot_general(a, b, NT, preferred_element_type=F32)


def dot_tn(a, b):
    return lax.dot_general(a, b, TN, preferred_element_type=F32)


def mark(hit):
    return jnp.where(hit, 1.0, 0.0).astype(BF)


def split(a):
    high = a.astype(BF)
    return high, (a - high.astype(F32)).astype(BF)


def along(z):
    half = (z + 1) // 2
    return [k % 2 * half + k // 2 for k in range(z)]


def in_order(blocks_ref):
    z = blocks_ref.shape[0]
    places = along(z)
    return jnp.concatenate([blocks_ref[places.index(k)] for k in range(z)], axis=0)


def exchange_z(blocks):
    return lax.all_to_all(
        blocks, "z", 0, 0, tiled=True, axis_index_groups=[along(blocks.shape[0])]
    )


def send_kernel(order_hbm, rows_hbm, out_ref, order_ref, rows_ref, sems):
    order_copy = pltpu.make_async_copy(order_hbm, order_ref, sems.at[0])
    rows_copy = pltpu.make_async_copy(rows_hbm, rows_ref, sems.at[1])
    order_copy.start()
    rows_copy.start()
    order_copy.wait()
    n = rows_ref.shape[0]
    places = mark(lax.broadcasted_iota(jnp.int32, (n, n), 0) == order_ref[...])
    rows_copy.wait()
    sent = dot_tn(places, rows_ref[...]).astype(BF)
    z, share, _ = out_ref.shape
    for k, device in enumerate(along(z)):
        out_ref[k] = sent[device * share : (device + 1) * share]


def local_kernel(count_ref, nodes_ref, edges_ref, cot_ref, w2_ref, high_ref, low_ref, t_ref):
    most, tile = nodes_ref.shape
    n = cot_ref.shape[0]
    count = count_ref[0, 0]
    ids = lax.broadcasted_iota(jnp.int32, (n, tile), 0)
    total = jnp.zeros((n, n), F32)
    for b in range(most):
        used = jnp.where(b < count, 1.0, 0.0)
        at = mark(ids == nodes_ref[b : b + 1, :])
        edges = (edges_ref[b].astype(F32) * used).astype(BF)
        total = total + dot_nt(dot(at, edges).astype(BF), at)
    high, low = split(total)
    high_ref[...] = high
    low_ref[...] = low
    dagg = dot_nt(cot_ref[...], w2_ref[...]).astype(BF)
    t_ref[...] = dot_tn(high, dagg) + dot_tn(low, dagg)


def node_kernel(factor, core_ref, part_ref, w1_ref, cot_ref, high_ref, low_ref, t_ref, send_ref, g_ref, m_ref):
    part = in_order(part_ref)
    pre = dot(part, w1_ref[...])
    sig = jax.nn.sigmoid(pre)
    act = (pre * sig).astype(BF)
    g = (t_ref[...] * sig * (1.0 + pre * (1.0 - sig))).astype(BF)
    m = (dot(high_ref[...], act) + dot(low_ref[...], act)).astype(BF)
    g_ref[...] = g
    m_ref[...] = m
    zeroth = core_ref[0, 0] == 0

    @pl.when(zeroth)
    def _():
        send_ref[...] = (dot_tn(m, cot_ref[...]) * factor).astype(BF)

    @pl.when(jnp.logical_not(zeroth))
    def _():
        send_ref[...] = (dot_tn(part, g) * factor).astype(BF)


def keep_kernel(factor, core_ref, part_ref, w1_ref, cot_ref, g_ref, m_ref, keep_ref, dpart_ref):
    zeroth = core_ref[0, 0] == 0
    g = g_ref[...]

    @pl.when(zeroth)
    def _():
        keep_ref[...] = dot_tn(in_order(part_ref), g) * factor

    @pl.when(jnp.logical_not(zeroth))
    def _():
        keep_ref[...] = dot_tn(m_ref[...], cot_ref[...]) * factor

    dpart_ref[...] = dot_nt(g, w1_ref[...]).astype(BF)


def add_kernel(keep_ref, got_ref, out_ref):
    nx, ny, share, _ = out_ref.shape
    for k, y in enumerate(along(ny)):
        for x in range(nx):
            at = pl.ds((y * nx + x) * share, share)
            out_ref[x, k] = (keep_ref[at, :] + got_ref[at, :].astype(F32)).astype(BF)


def sum_x_kernel(pieces_ref, out_ref):
    out_ref[...] = jnp.sum(pieces_ref[...].astype(F32), axis=0).astype(BF)


def sum_kernel(pieces_ref, dpart_ref, both_ref):
    z, share, _ = dpart_ref.shape
    total = jnp.sum(pieces_ref[...].astype(F32), axis=0).astype(BF)
    for k, device in enumerate(along(z)):
        both_ref[k, 0:share, :] = dpart_ref[device]
        both_ref[k, share:, :] = total


def spread_kernel(both_ref, back_ref, whole_ref):
    z, share, _ = back_ref.shape
    for k, device in enumerate(along(z)):
        back_ref[device] = both_ref[k, 0:share, :]
    total = jnp.sum(both_ref[:, share:, :].astype(F32), axis=0).astype(BF)
    for k in range(whole_ref.shape[0]):
        whole_ref[k] = total


def place_kernel(order_ref, back_ref, out_ref):
    n = back_ref.shape[0]
    places = mark(lax.broadcasted_iota(jnp.int32, (n, n), 0) == order_ref[...])
    out_ref[...] = dot(places, back_ref[...]).astype(BF)


def final_kernel(plane, core_ref, mine_ref, other_ref, first_ref, second_ref):
    zeroth = core_ref[0, 0] == 0
    d = mine_ref.shape[0]
    share = d // plane
    for k, device in enumerate(along(plane)):
        at, to = pl.ds(k * share, share), pl.ds(device * share, share)
        mine, other = mine_ref[at, :].astype(F32), other_ref[at, :].astype(F32)
        first_ref[to, :] = jnp.where(zeroth, mine, other)
        second_ref[to, :] = jnp.where(zeroth, other, mine)


def call(kernel, out_shape, flops, nbytes, *args, smem=0):
    specs = [pl.BlockSpec(memory_space=pltpu.SMEM)] * smem
    specs += [pl.BlockSpec(memory_space=pltpu.VMEM)] * (len(args) - smem)
    return pl.pallas_call(
        kernel,
        out_shape=out_shape,
        in_specs=specs,
        compiler_params=pltpu.CompilerParams(vmem_limit_bytes=32 * 1024 * 1024),
        cost_estimate=pl.CostEstimate(flops=flops, bytes_accessed=nbytes, transcendentals=0),
    )(*args)


def shards(grid, cotangent, send_order, tile_nodes, tile_edges, tile_count, w_first, w_second):
    rows, cot, order = grid[0, 0], cotangent[0, 0], send_order[0]
    nodes, edges = tile_nodes[0, 0], tile_edges[0, 0]
    z = lax.axis_size("z")
    plane = lax.axis_size("y") * lax.axis_size("x")
    rep = plane * lax.axis_size("c")
    core = lax.axis_index("c").reshape(1, 1)
    swap = [(0, 1), (1, 0)]
    n, d = rows.shape
    most, tile = nodes.shape
    factor = float(z * rep * most * tile) ** -0.5
    sd = jax.ShapeDtypeStruct

    outgoing = pl.pallas_call(
        send_kernel,
        out_shape=sd((z, n // z, d), BF),
        in_specs=[pl.BlockSpec(memory_space=pl.ANY)] * 2,
        out_specs=pl.BlockSpec(memory_space=pltpu.VMEM),
        scratch_shapes=[
            pltpu.VMEM((1, n), jnp.int32),
            pltpu.VMEM((n, d), BF),
            pltpu.SemaphoreType.DMA((2,)),
        ],
    )(order, rows)
    part = exchange_z(outgoing)

    high, low, t = call(
        local_kernel,
        (sd((n, n), BF), sd((n, n), BF), sd((n, d), F32)),
        10**9, 6 * 10**6, tile_count, nodes, edges, cot, w_second, smem=1,
    )
    send, g, m = call(
        lambda *refs: node_kernel(factor, *refs),
        (sd((d, d), BF), sd((n, d), BF), sd((n, d), BF)),
        4 * 10**8, 3 * 10**6, core, part, w_first, cot, high, low, t, smem=1,
    )
    got = lax.ppermute(send, "c", swap)
    keep, dpart = call(
        lambda *refs: keep_kernel(factor, *refs),
        (sd((d, d), F32), sd((n, d), BF)),
        2 * 10**8, 3 * 10**6, core, part, w_first, cot, g, m, smem=1,
    )
    nx = lax.axis_size("x")
    share = d // plane
    grad = call(
        add_kernel, sd((nx, plane // nx, share, d), BF), 10**6, 2 * 10**6, keep, got
    )
    grad = lax.all_to_all(grad.reshape(nx, d // nx, d), "x", 0, 0, tiled=True)
    grad = call(sum_x_kernel, sd((d // nx, d), BF), 10**6, 10**6, grad)
    pieces = lax.all_to_all(
        grad.reshape(plane // nx, share, d), "y", 0, 0, tiled=True, axis_index_groups=[along(plane // nx)]
    )
    both = call(
        sum_kernel, sd((z, n // z + share, d), BF), 10**6, 2 * 10**6,
        pieces, dpart.reshape(z, n // z, d),
    )
    both = exchange_z(both)
    back, whole = call(
        spread_kernel, (sd((z, n // z, d), BF), sd((plane, share, d), BF)), 10**6, 2 * 10**6, both
    )
    mine = lax.all_to_all(
        whole, ("y", "x"), 0, 0, tiled=True, axis_index_groups=[along(plane)]
    ).reshape(d, d)
    grad_rows = call(
        place_kernel, sd((n, d), BF), 2 * n * n * d, 4 * n * d, order, back.reshape(n, d)
    )
    other = lax.ppermute(mine, "c", swap)
    first, second = call(
        lambda *refs: final_kernel(plane, *refs), (sd((d, d), F32), sd((d, d), F32)), 10**6, 3 * 10**6,
        core, mine, other, smem=1,
    )
    return (grad_rows[None, None], first, second)


def solution(mesh):
    z, rep = mesh.shape["grp"], mesh.shape["rep"]
    mesh = Mesh(mesh.devices.reshape(z, rep // 8, 4, 2), ("z", "y", "x", "c"))
    group = ("y", "x", "c")
    in_specs = (
        P(group, "z", None, None),
        P(group, "z", None, None),
        P(group, "z", None),
        P(group, "z", None, None),
        P(group, "z", None, None, None),
        P(group, "z"),
        P(),
        P(),
    )
    out_specs = (P(group, "z", None, None), P(), P())
    return jax.shard_map(shards, mesh=mesh, in_specs=in_specs, out_specs=out_specs, check_vma=False)
```
